256 devices in a mesh: dp: 8 (over x, core), expert: 32 (over z, y).
Axes of the slice: x: 4, y: 4, z: 8, core: 2. Of those that a mesh axis runs over, the one named last changes fastest.
Arguments:
- tokens: bfloat16 [2, 1536, 7168], P(None, 'expert'), may hold values from -6 to 6
- routes: int32 [2, 1536, 4], P(None, 'expert'), may hold values from 0 to 31, all different within a row; in each aligned block of 48 rows (0 to 47, 48 to 95, ..., all dimensions but the last counted through in order) at most 9 rows name the same one
- route_weights: float32 [2, 1536, 4], P(None, 'expert'), may hold values from 0.1 to 1
- domains: int32 [2, 1536], P(None, 'expert'), may hold values from 0 to 3
- gate_weight: bfloat16 [32, 7168, 2048], P('expert', None, 'dp'), may hold values from -0.0625 to 0.0625
- up_weight: bfloat16 [32, 7168, 2048], P('expert', None, 'dp'), may hold values from -0.0625 to 0.0625
- down_weight: bfloat16 [32, 2048, 7168], P('expert', 'dp'), may hold values from -0.1875 to 0.1875
- up_entry: bfloat16 [32, 7168, 128], P('expert', 'dp'), may hold values from -0.0625 to 0.0625
- up_exit: bfloat16 [32, 128, 2048], P('expert', None, 'dp'), may hold values from -1 to 1
- down_entry: bfloat16 [32, 2048, 128], P('expert', 'dp'), may hold values from -0.125 to 0.125
- down_exit: bfloat16 [32, 128, 7168], P('expert', None, 'dp'), may hold values from -1 to 1
Outputs:
- mixed: bfloat16 [2, 1536, 7168], P(None, 'expert', 'dp')
The draws below stay inside these ranges and needn't reach their ends.
Inputs may be any that keep to these rules, and one draw needn't show every extreme that they name: `routes`: each row names 4 different experts. Among the 48 tokens of one index of expert in one step, no expert is named by more than 9 rows, a bound that some block reaches.
All inputs are finite; a program needn't handle non-finite values.
Results may differ from the reference program's by a relative error of at most 0.027.
Values may be sent and summed in bfloat16 or wider, within the bound.
A program may use at most 128 MiB of HBM per device.

```python
import math
import jax
import jax.numpy as jnp
import numpy as np
from jax import lax

D = 7168
FF = 2048
TOP = 4
RANK = 32
DOMAINS = 4
STEPS = 2
TOK_DEV = 48
EXPERTS = 32
CAP = 9
TOKENS = 1536
N_DP = 8


def place_ends(result, stream_key, smallest, largest):
    longest = result.shape.index(max(result.shape))
    spots = []
    for shift in (0, 1):
        where = [jax.random.randint(jax.random.fold_in(stream_key, axis), (), 0, length) for axis, length in enumerate(result.shape)]
        where[longest] = (where[longest] + shift) % result.shape[longest]
        spots.append(tuple(where))
    return result.at[spots[0]].set(smallest).at[spots[1]].set(largest)


def raised(drawn, rng, source, target, shards_of, factor):
    def block_of(dim):
        return (jnp.arange(drawn.shape[dim]) // (drawn.shape[dim] // shards_of)).reshape((-1,) + (1,) * (drawn.ndim - 1 - dim))

    first = jax.random.permutation(rng, shards_of)[block_of(target)]
    far = (block_of(target) + shards_of // 2) % shards_of
    return jnp.where((block_of(source) == first) | (block_of(source) == far), factor * drawn, drawn)


def block_levels(stream_key, shape, pieces, least, top_value):
    loudness = 1.0
    for dim, parts in pieces:
        steps = jax.random.uniform(jax.random.fold_in(jax.random.fold_in(stream_key, 6), dim), (parts,), jnp.float32, least / len(pieces), top_value / len(pieces))
        loudness = loudness * jnp.repeat(jnp.exp(steps), shape[dim] // parts).reshape((-1,) + (1,) * (len(shape) - 1 - dim))
    return loudness


def shared_out(key, own, number, rows, number_of, top, most, skew):
    sequence = jax.random.permutation(key, number_of)
    crowded, usual = portions_of(number_of, rows * top, most, skew, True), portions_of(number_of, rows * top, most, skew, False)
    places = jnp.arange(number_of)

    def named(sizes, rotation):
        used = int((sizes > 0).sum())
        fixed = max(1, used // 4)
        shifted = fixed + (places - fixed + rotation * (used - fixed)) % max(1, number_of - fixed)
        return jnp.zeros((number_of,), jnp.int32).at[sequence[jnp.where(places < fixed, places, shifted)]].set(jnp.asarray(sizes, jnp.int32))

    sizes = jnp.where(number % 4 == 0, named(crowded, number // 4), named(usual, number - number // 4 - 1))
    mixed = jax.random.permutation(jax.random.fold_in(own, 3), number_of)
    source_of, receiver = mixed[0:number_of // 2 * 2:2], mixed[1:number_of // 2 * 2:2]
    room = jnp.minimum(sizes[source_of] - 1, most - sizes[receiver]) // 2
    room = jnp.where((source_of == sequence[0]) | (receiver == sequence[0]) | (sizes[receiver] == 0), 0, jnp.maximum(room, 0))
    shifted = jax.random.randint(jax.random.fold_in(own, 4), (number_of // 2,), 0, 1 << 20) % (room + 1)
    sizes = sizes.at[source_of].add(-shifted).at[receiver].add(shifted)
    labels = jnp.searchsorted(jnp.cumsum(sizes), jnp.arange(rows * top), side="right").astype(jnp.int32)
    grid = labels.reshape(top, rows).T
    grid = grid[jax.random.permutation(jax.random.fold_in(own, 1), rows)]
    rotation = jax.random.randint(jax.random.fold_in(own, 2), (rows, 1), 0, top)
    return jnp.take_along_axis(grid, (jnp.arange(top)[None, :] + rotation) % top, axis=1)


def portions_of(amount, total, reach, skew, full):
    portions = [(1 << 20) // math.isqrt(standing ** skew) + 1 for standing in range(1, amount + 1)]
    largest = reach if full else min(reach, max(-(-total // amount), total * portions[0] // sum(portions)))
    least = 1 if total - largest >= amount - 1 else 0
    given, rest = [largest] + [least] * (amount - 1), total - largest - least * (amount - 1)
    while rest > 0:
        movable = [i for i in range(1, amount) if given[i] < largest] or [i for i in range(1, amount) if given[i] < reach]
        whole, budget = sum([portions[i] for i in movable]), rest
        for i in movable:
            extra = min(reach - given[i], max(1, budget * portions[i] // whole), rest)
            given[i] = given[i] + extra
            rest = rest - extra
    return np.array(given)


def bell_draw(stream_key, extent, scale, bound, split=(), kind=jnp.bfloat16):
    loudness = block_levels(stream_key, extent, split, -0.22, 0.18) if split else 1.0
    values = jax.random.normal(stream_key, extent, jnp.float32) * scale * loudness
    return jnp.minimum(jnp.maximum(values, -bound), bound).astype(kind)


def bell_draw_with(rng, extent, scale, most, pieces, heavy, kind=jnp.bfloat16):
    array = scale * jax.random.normal(rng, extent, jnp.float32)
    if pieces:
        array = array * block_levels(rng, extent, pieces, -0.22, 0.18)
    return jnp.clip(raised(array, jax.random.fold_in(rng, 3), *heavy), -most, most).astype(kind)


def setup_inputs(seed: int = 0) -> dict:
    keys = jax.random.split(jax.random.key(seed), 12)
    tokens = bell_draw(keys[0], (STEPS, TOKENS, D), 1.0, 6.0, ((1, 32),))
    routes_keys = jax.random.split(jax.random.fold_in(keys[1], 1), STEPS * TOKENS // TOK_DEV)
    routes_turns = jax.random.permutation(jax.random.fold_in(keys[1], 3), STEPS * TOKENS // TOK_DEV)
    routes = jax.vmap(lambda own, number: shared_out(jax.random.fold_in(keys[1], 2), own, number, TOK_DEV, EXPERTS, TOP, CAP, 1))(routes_keys, routes_turns).reshape((STEPS, TOKENS, TOP))
    route_weights = jnp.clip(jnp.exp(math.log(1.0) - 2.3025851 * jax.random.uniform(keys[2], (STEPS, TOKENS, TOP), jnp.float32) ** block_levels(keys[2], (STEPS, TOKENS, TOP), ((1, 32),), -0.2, 0.2)), 0.1, 1.0)
    domains = place_ends(jax.random.randint(keys[3], (STEPS, TOKENS), 0, DOMAINS), jax.random.fold_in(keys[3], 1), 0, DOMAINS - 1).astype(jnp.int32)
    gate_weight = bell_draw(keys[4], (EXPERTS, D, FF), D ** -0.5, 0.0625, ((0, 32), (2, 8)))
    up_weight = bell_draw(keys[5], (EXPERTS, D, FF), D ** -0.5, 0.0625, ((0, 32), (2, 8)))
    down_weight = bell_draw_with(keys[6], (EXPERTS, FF, D), FF ** -0.5, 0.1875, ((0, 32), (1, 8)), (1, 2, 8, 2.0))
    up_entry = bell_draw(keys[7], (EXPERTS, D, DOMAINS * RANK), D ** -0.5, 0.0625, ((0, 32), (1, 8)))
    up_exit = bell_draw(keys[8], (EXPERTS, DOMAINS * RANK, FF), RANK ** -0.5, 1.0, ((0, 32), (2, 8)))
    down_entry = bell_draw(keys[9], (EXPERTS, FF, DOMAINS * RANK), FF ** -0.5, 0.125, ((0, 32), (1, 8)))
    down_exit = bell_draw(keys[10], (EXPERTS, DOMAINS * RANK, D), RANK ** -0.5, 1.0, ((0, 32), (2, 8)))
    return {"tokens": tokens, "routes": routes, "route_weights": route_weights, "domains": domains, "gate_weight": gate_weight, "up_weight": up_weight, "down_weight": down_weight, "up_entry": up_entry, "up_exit": up_exit, "down_entry": down_entry, "down_exit": down_exit}


def expert_output(routed, routed_hot, gate_local, up_local, down_local, up_enter, up_leave, down_enter, down_leave):
    group_width = FF // N_DP
    part_width = D // N_DP
    count_rows = routed.shape[0]
    domain_mask = jnp.repeat(routed_hot, RANK, axis=1)
    gate_sum = jnp.dot(routed, gate_local, preferred_element_type=jnp.float32)
    low_rank = (jnp.dot(routed, up_enter, preferred_element_type=jnp.float32) * domain_mask).astype(jnp.bfloat16)
    up_sum = jnp.dot(routed, up_local, preferred_element_type=jnp.float32) + jnp.dot(low_rank, up_leave, preferred_element_type=jnp.float32)
    hidden = (jax.nn.silu(gate_sum) * up_sum).astype(jnp.bfloat16)
    low_down = (jnp.dot(hidden, down_enter, preferred_element_type=jnp.float32) * domain_mask).astype(jnp.bfloat16)
    adapter = jnp.dot(low_down, down_leave, preferred_element_type=jnp.float32).reshape(count_rows, N_DP, part_width)
    block_eye = jnp.eye(N_DP, dtype=jnp.float32)
    placed = (block_eye[:, None, :, None] * adapter[None]).reshape(N_DP, count_rows, D)
    partial_value = jnp.einsum("mgh,ghd->gmd", hidden.astype(jnp.float32).reshape(count_rows, N_DP, group_width),
                         down_local.astype(jnp.float32).reshape(N_DP, group_width, D),
                         precision=lax.Precision.HIGHEST)
    rounded = lax.optimization_barrier((partial_value + placed).astype(jnp.bfloat16))
    return jnp.sum(rounded.astype(jnp.float32), axis=0)


def reference(tokens, routes, route_weights, domains, gate_weight, up_weight, down_weight, up_entry, up_exit, down_entry, down_exit):
    slot_count = EXPERTS * CAP
    mixed_steps = []
    for step_index in range(STEPS):
        chosen = routes[step_index].reshape(-1).astype(jnp.int32)
        pair_count = chosen.shape[0]
        onehot = (chosen[:, None] == jnp.arange(EXPERTS, dtype=jnp.int32)[None, :]).astype(jnp.int32)
        slot_rank = jnp.sum((jnp.cumsum(onehot, axis=0) - onehot) * onehot, axis=1).astype(jnp.int32)
        owners = (jnp.arange(pair_count, dtype=jnp.int32) // TOP).astype(jnp.int32)
        slot_source = jnp.zeros((EXPERTS, slot_count), jnp.int32).at[chosen, slot_rank].set(owners)
        slot_filled = jnp.zeros((EXPERTS, slot_count), jnp.float32).at[chosen, slot_rank].set(1.0)
        inputs = tokens[step_index]
        domain_hot = (domains[step_index][:, None] == jnp.arange(DOMAINS, dtype=jnp.int32)[None, :]).astype(jnp.float32)

        def per_expert(packed):
            source_rows, filled, gate_local, up_local, down_local, up_enter, up_leave, down_enter, down_leave = packed
            routed = inputs[source_rows] * filled[:, None].astype(jnp.bfloat16)
            routed_hot = domain_hot[source_rows] * filled[:, None]
            return expert_output(routed, routed_hot, gate_local, up_local, down_local, up_enter, up_leave, down_enter, down_leave)

        outputs = lax.map(per_expert, (slot_source, slot_filled, gate_weight, up_weight, down_weight, up_entry, up_exit, down_entry, down_exit))
        picked = outputs[chosen, slot_rank].reshape(TOKENS, TOP, D)
        combined = jnp.sum(picked * route_weights[step_index][:, :, None], axis=1)
        mixed_steps.append(combined.astype(jnp.bfloat16))
    return jnp.stack(mixed_steps)
```

```python
import jax
import jax.numpy as jnp
from jax import lax
from jax.experimental import pallas as pl
from jax.experimental.pallas import tpu as pltpu
from jax.sharding import PartitionSpec as P

MESH = pl.DeviceIdType.MESH
F32 = jnp.float32
BF16 = jnp.bfloat16

TOP = 4
RANK = 32
DOMAINS = 4
STEPS = 2
TOK = 48
CAP = 9
EXPERTS = 32
D = 7168
FFL = 256
PART = 896
LOW = RANK * DOMAINS
NX, NY, NZ = 4, 4, 8
SLOT = STEPS * CAP
ROWS = NY * SLOT
PAD = 80
ALL = NZ * ROWS
HALF = ALL // 2
BLOCK = STEPS * TOK
CHUNKS = ((0, 256), (256, 256), (512, 256), (768, 128))
NC = len(CHUNKS)
W = 256


def dot(a, b):
    return jnp.dot(a, b, preferred_element_type=F32)


def kernel(
    tokens, table, domhot, gate, up, down, up_enter, up_leave, down_enter, down_leave,
    out,
    wgu, wd, g, tab, sel, selwt, zs, zr, xg, mask, acc, hid,
    sb, sr, ss, hr, tr, tp, vz, own, ys, yr,
    load_sem, ysend, yrecv, tsend, trecv, zsend, zrecv, xsend, xrecv,
    wsend, wrecv, bsend, brecv, hsend, hrecv, rsend, rrecv, vsend, vrecv, osend, orecv,
):
    dp = lax.axis_index("dp")
    ex = lax.axis_index("expert")
    x, core = dp // 2, dp % 2
    z, y = ex // NY, ex % NY
    sib = x * 2 + (1 - core)
    ip, im, io = (x + 1) % NX, (x + 3) % NX, (x + 2) % NX
    xp, xm, xo = ip * 2 + core, im * 2 + core, io * 2 + core

    def at_y(m):
        return z * NY + (y + m) % NY

    def at_z(k):
        return ((z + k) % NZ) * NY + y

    def send(src, dst, ssem, rsem, **where):
        return pltpu.make_async_remote_copy(
            src_ref=src, dst_ref=dst, send_sem=ssem, recv_sem=rsem,
            device_id=where, device_id_type=MESH,
        )

    barrier = pltpu.get_barrier_semaphore()
    for peer in (xp, xm, sib):
        pl.semaphore_signal(barrier, inc=1, device_id={"dp": peer}, device_id_type=MESH)
    for m in range(1, NY):
        pl.semaphore_signal(barrier, inc=1, device_id={"expert": at_y(m)}, device_id_type=MESH)
    for k in range(1, NZ):
        pl.semaphore_signal(barrier, inc=1, device_id={"expert": at_z(k)}, device_id_type=MESH)

    token_loads = []
    for c, (off, wide) in enumerate(CHUNKS):
        for s in range(STEPS):
            token_loads.append(
                pltpu.make_async_copy(
                    tokens.at[s, :, pl.ds(pl.multiple_of(dp * PART + off, 128), wide)],
                    g.at[c, 0, pl.ds(s * TOK, TOK), pl.ds(0, wide)],
                    load_sem.at[c * STEPS + s],
                )
            )
    token_loads.append(
        pltpu.make_async_copy(
            domhot, g.at[NC - 1, 0, pl.ds(0, BLOCK), pl.ds(128, 128)], load_sem.at[8]
        )
    )
    my_rows = pl.ds(pl.multiple_of(dp * PART, 128), PART)
    weight_loads = [
        pltpu.make_async_copy(up_enter, wgu.at[my_rows, pl.ds(512, LOW)], load_sem.at[9]),
        pltpu.make_async_copy(down_leave, wd.at[pl.ds(FFL, LOW), my_rows], load_sem.at[10]),
        pltpu.make_async_copy(gate, wgu.at[:, pl.ds(0, FFL)], load_sem.at[11]),
        pltpu.make_async_copy(up, wgu.at[:, pl.ds(FFL, FFL)], load_sem.at[12]),
        pltpu.make_async_copy(down, wd.at[pl.ds(0, FFL), :], load_sem.at[13]),
    ]
    for copy in token_loads + weight_loads:
        copy.start()
    for c in range(NC):
        for m in range(NY):
            g[c, m, BLOCK:, :] = jnp.zeros((128 - BLOCK, W), BF16)
    for cc in range(NC):
        for k in range(NZ):
            vz[cc, k, PAD:, :] = jnp.zeros((128 - PAD, W), BF16)
    pl.semaphore_wait(barrier, 13)

    def table_copy(m):
        return send(
            table.at[(y + m) % NY], tab.at[m], tsend.at[m], trecv.at[m], expert=at_y(m)
        )

    def y_copy(c, m):
        i = c * NY + m
        return send(
            g.at[c, 0, pl.ds(0, BLOCK)], g.at[c, m, pl.ds(0, BLOCK)],
            ysend.at[i], yrecv.at[i], expert=at_y(m),
        )

    for m in range(1, NY):
        table_copy(m).start()
    for copy in token_loads:
        copy.wait()
    for c in range(NC):
        for m in range(1, NY):
            y_copy(c, m).start()

    def spread(block, ssem, rsem, base, first, second):
        def near(kind, to, who):
            return send(block(who, 0), block(who, 0), ssem.at[base + kind], rsem.at[base + kind], dp=to)

        def far(kind, to, who):
            return send(
                block(who, kind - 2), block(who, kind - 2),
                ssem.at[base + kind], rsem.at[base + kind], dp=to,
            )

        if first:
            near(0, xp, dp).start()
            near(1, xm, dp).start()
            near(2, sib, dp).start()
        if second == "middle":
            near(0, xp, xm).wait_recv()
            far(3, xp, xm).start()
            near(5, sib, xm).start()
            near(1, xm, xp).wait_recv()
            far(4, xm, xp).start()
            near(6, sib, xp).start()
        if second == "end":
            far(3, xp, xo).wait_recv()
            far(4, xm, xo).wait_recv()
            near(7, sib, xo).start()
        if second == "all":
            for kind, step in ((2, 0), (5, 3), (6, 1), (7, 2)):
                near(kind, sib, ((x + step) % NX) * 2 + 1 - core).wait_recv()
        if second == "sent":
            for kind in (0, 1, 2, 5, 6, 7):
                near(kind, sib, dp).wait_send()
            far(3, xp, dp).wait_send()
            far(4, xm, dp).wait_send()

    def enter_block(who, part):
        start, size = ((0, PART), (0, PART // 2), (PART // 2, PART // 2))[part]
        return wgu.at[pl.ds(pl.multiple_of(who * PART + start, 64), size), pl.ds(512, LOW)]

    def leave_block(who, part):
        start, size = ((0, LOW), (0, LOW // 2), (LOW // 2, LOW // 2))[part]
        return wd.at[pl.ds(FFL + start, size), pl.ds(pl.multiple_of(who * PART, 128), PART)]

    def token_block(c):
        wide = CHUNKS[c][1]

        def block(who, part):
            start, size = ((0, ALL), (0, HALF), (HALF, HALF))[part]
            return xg.at[c, who, pl.ds(start, size), pl.ds(0, wide)]

        return block

    def weights(first, second):
        spread(enter_block, wsend, wrecv, 0, first, second)
        spread(leave_block, wsend, wrecv, 8, first, second)

    def gather(c, first, second):
        spread(token_block(c), xsend, xrecv, c * 8, first, second)

    weight_loads[0].wait()
    weight_loads[1].wait()
    weights(True, None)

    for m in range(1, NY):
        table_copy(m).wait_recv()

    def choose(k, carry):
        zd = (z + k) % NZ
        for m in range(NY):
            if m == 0:
                code, weight = table[y, pl.ds(zd, 1), :], table[y, pl.ds(NZ + zd, 1), :]
            else:
                code, weight = tab[m, pl.ds(zd, 1), :], tab[m, pl.ds(NZ + zd, 1), :]
            code = jnp.where(code >= 0.0, code + float(SLOT * m), -1.0)
            at = lax.broadcasted_iota(jnp.int32, (128, 128), 0).astype(F32) == code
            hot = jnp.where(at, 1.0, 0.0)
            sel[pl.ds(pl.multiple_of(k * PAD, 16), PAD), m * 128 : (m + 1) * 128] = hot[
                :PAD
            ].astype(BF16)
            selwt[m * 128 : (m + 1) * 128, pl.ds(pl.multiple_of(k * 128, 128), 128)] = (
                jnp.where(at, weight, 0.0).T.astype(BF16)
            )
        return carry

    lax.fori_loop(0, NZ, choose, 0)

    def z_copy(c, k):
        i = c * NZ + k
        return send(zs.at[c, k], zr.at[c, k], zsend.at[i], zrecv.at[i], expert=at_z(k))

    def stage_b(c):
        for m in range(1, NY):
            y_copy(c, m).wait_recv()
        rows = dot(sel[...], g[c].reshape(NY * 128, W)).astype(BF16).reshape(NZ, PAD, W)
        zs[c] = rows
        for k in range(1, NZ):
            z_copy(c, k).start()
        zr[c, 0] = rows[0]

    def stage_c(c):
        for k in range(1, NZ):
            z_copy(c, k).wait_recv()
        rows = zr[c].astype(F32)[:, :ROWS].reshape(ALL, W).astype(BF16)
        if c < NC - 1:
            xg[c, dp] = rows
        else:
            xg[c, dp, :, :128] = rows[:, :128]
            mask[...] = rows[:, 128:]
        gather(c, True, None)

    def stage_e(c):
        gather(c, False, "end")
        gather(c, False, "all")
        off, wide = CHUNKS[c]

        def part(shard, carry):
            depth = pl.ds(pl.multiple_of(shard * PART + off, 128), wide)
            term = dot(xg[c, shard, :, :wide], wgu[depth, :])
            acc[...] += term
            return carry

        lax.fori_loop(0, 2 * NX, part, 0)

    acc[...] = jnp.zeros_like(acc)
    stage_b(0)
    stage_b(1)
    weights(False, "middle")
    stage_c(0)
    stage_b(2)
    weights(False, "end")
    stage_c(1)
    gather(0, False, "middle")
    stage_b(3)
    stage_c(2)
    gather(1, False, "middle")
    weights(False, "all")
    for copy in weight_loads[2:]:
        copy.wait()
    stage_e(0)
    stage_c(3)
    gather(2, False, "middle")
    stage_e(1)
    gather(3, False, "middle")
    stage_e(2)
    stage_e(3)

    domain = mask[...].astype(F32)
    low = (acc[:, 2 * FFL :] * domain).astype(BF16)
    gated = acc[:, :FFL]
    upped = acc[:, FFL : 2 * FFL] + dot(low, up_leave[...])
    hidden = (gated / (1.0 + jnp.exp(-gated)) * upped).astype(BF16)
    hid[:, :FFL] = hidden
    hid[:, FFL:] = (dot(hidden, down_enter[...]) * domain).astype(BF16)

    def partial(cc, shard):
        off, wide = CHUNKS[cc]
        return dot(hid[...], wd[:, pl.ds(pl.multiple_of(shard * PART + off, 128), wide)])

    def b_copy(cc, i):
        wide = CHUNKS[cc][1]
        n = cc * NX + i
        return send(
            sb.at[cc, i, :, pl.ds(0, wide)], sr.at[cc, i, :, pl.ds(0, wide)],
            bsend.at[n], brecv.at[n], dp=sib,
        )

    def h_copy(cc, i):
        wide = CHUNKS[cc][1]
        n = cc * 2 + i
        return send(
            ss.at[cc, 2, pl.ds(i * HALF, HALF), pl.ds(0, wide)],
            hr.at[cc, i, :, pl.ds(0, wide)],
            hsend.at[n], hrecv.at[n], dp=(xp, xm)[i],
        )

    def r_copy(cc, i):
        wide = CHUNKS[cc][1]
        n = cc * 2 + i
        return send(
            ss.at[cc, i, :, pl.ds(0, wide)], tr.at[cc, i, :, pl.ds(0, wide)],
            rsend.at[n], rrecv.at[n], dp=(xp, xm)[i],
        )

    def v_copy(cc, k):
        wide = CHUNKS[cc][1]
        n = cc * NZ + k
        return send(
            tp.at[cc, k, :, pl.ds(0, wide)], vz.at[cc, k, pl.ds(0, PAD), pl.ds(0, wide)],
            vsend.at[n], vrecv.at[n], expert=at_z(NZ - k),
        )

    def o_copy(cc, m):
        wide = CHUNKS[cc][1]
        n = cc * NY + m
        return send(
            ys.at[cc, m, :, pl.ds(0, wide)], yr.at[cc, m, :, pl.ds(0, wide)],
            osend.at[n], orecv.at[n], expert=at_y(NY - m),
        )

    def paired(cc, i):
        wide = CHUNKS[cc][1]
        b_copy(cc, i).wait_recv()
        return partial(cc, i * 2 + core) + sr[cc, i, :, :wide].astype(F32)

    def stage_1(cc):
        wide = CHUNKS[cc][1]

        def one(j, carry):
            i = (x + 2 + j) % NX
            sb[cc, i, :, :wide] = partial(cc, i * 2 + 1 - core).astype(BF16)
            b_copy(cc, i).start()
            return carry

        lax.fori_loop(0, NX, one, 0)

    def stage_2(cc):
        ss[cc, 2, :, : CHUNKS[cc][1]] = paired(cc, io).astype(BF16)
        h_copy(cc, 0).start()
        h_copy(cc, 1).start()

    def stage_3(cc):
        wide = CHUNKS[cc][1]
        for i, to in enumerate((ip, im)):
            total = paired(cc, to)
            h_copy(cc, i).wait_recv()
            more = hr[cc, i, :, :wide].astype(F32)
            if i == 0:
                ss[cc, 0, :HALF, :wide] = (total[:HALF] + more).astype(BF16)
                ss[cc, 0, HALF:, :wide] = total[HALF:].astype(BF16)
            else:
                ss[cc, 1, :HALF, :wide] = total[:HALF].astype(BF16)
                ss[cc, 1, HALF:, :wide] = (total[HALF:] + more).astype(BF16)
            r_copy(cc, i).start()

    def stage_4(cc):
        wide = CHUNKS[cc][1]
        total = paired(cc, x)
        for i in range(2):
            r_copy(cc, i).wait_recv()
            total = total + tr[cc, i, :, :wide].astype(F32)
        total = total.reshape(NZ, ROWS, wide)
        total = jnp.concatenate([total, jnp.zeros((NZ, PAD - ROWS, wide), F32)], axis=1)
        rows = total.astype(BF16)
        tp[cc, :, :, :wide] = rows
        for k in range(1, NZ):
            v_copy(cc, k).start()
        vz[cc, 0, :PAD, :wide] = rows[0]

    def stage_5(cc):
        wide = CHUNKS[cc][1]
        for k in range(1, NZ):
            v_copy(cc, k).wait_recv()
        rows = vz[cc, :, :, :wide].reshape(NZ * 128, wide)
        mixed = dot(selwt[...], rows).reshape(NY, 128, wide)[:, :BLOCK]
        for m in range(1, NY):
            ys[cc, m, :, :wide] = mixed[m].astype(BF16)
            o_copy(cc, m).start()
        own[cc, :, :wide] = mixed[0]

    def stage_6(cc):
        off, wide = CHUNKS[cc]
        total = own[cc, :, :wide]
        for m in range(1, NY):
            o_copy(cc, m).wait_recv()
            total = total + yr[cc, m, :, :wide].astype(F32)
        total = total.astype(BF16)
        for s in range(STEPS):
            out[s, :, off : off + wide] = total[s * TOK : (s + 1) * TOK]

    stages = (stage_1, stage_2, stage_3, stage_4, stage_5, stage_6)
    for stage, cc in (
        (1, 0), (1, 1), (2, 0), (2, 1), (3, 0), (1, 2), (2, 2), (3, 1), (4, 0), (1, 3), (2, 3),
        (3, 2), (4, 1), (5, 0), (3, 3), (4, 2), (5, 1), (6, 0), (4, 3), (5, 2), (6, 1),
        (5, 3), (6, 2), (6, 3),
    ):
        stages[stage - 1](cc)

    for m in range(1, NY):
        table_copy(m).wait_send()
    weights(False, "sent")
    for c in range(NC):
        for m in range(1, NY):
            y_copy(c, m).wait_send()
            o_copy(c, m).wait_send()
        for k in range(1, NZ):
            z_copy(c, k).wait_send()
            v_copy(c, k).wait_send()
        gather(c, False, "sent")
        for i in range(NX):
            b_copy(c, i).wait_send()
        for i in range(2):
            h_copy(c, i).wait_send()
            r_copy(c, i).wait_send()


def on_device(
    tokens,
    routes,
    route_weights,
    domains,
    gate_weight,
    up_weight,
    down_weight,
    up_entry,
    up_exit,
    down_entry,
    down_exit,
):
    experts = jnp.arange(EXPERTS, dtype=jnp.int32)
    named = routes[:, None, :, :] == experts[None, :, None, None]
    hit = jnp.sum(named.astype(F32), axis=3)
    weight = jnp.sum(jnp.where(named, route_weights[:, None, :, :], 0.0), axis=3)
    before = (jnp.arange(TOK)[:, None] < jnp.arange(TOK)[None, :]).astype(F32)
    rank = jnp.einsum("set,tu->seu", hit, before, preferred_element_type=F32)
    step = jnp.arange(STEPS, dtype=F32)[:, None, None]
    code = jnp.where(hit > 0, step * CAP + rank, -1.0)

    def arranged(array, fill):
        flat = jnp.transpose(array, (1, 0, 2)).reshape(NZ, NY, BLOCK)
        flat = jnp.transpose(flat, (1, 0, 2))
        return jnp.pad(flat, ((0, 0), (0, 0), (0, 128 - BLOCK)), constant_values=fill)

    table = jnp.concatenate([arranged(code, -1.0), arranged(weight, 0.0)], axis=1)
    domhot = (
        domains.reshape(BLOCK)[:, None] == (jnp.arange(LOW, dtype=jnp.int32) // RANK)[None, :]
    ).astype(BF16)

    any_spec = pl.BlockSpec(memory_space=pl.ANY)
    vmem_spec = pl.BlockSpec(memory_space=pltpu.VMEM)
    dma = pltpu.SemaphoreType.DMA
    vmem = pltpu.VMEM
    return pl.pallas_call(
        kernel,
        out_shape=jax.ShapeDtypeStruct((STEPS, TOK, PART), BF16),
        in_specs=[any_spec, vmem_spec] + [any_spec] * 5 + [vmem_spec, vmem_spec, any_spec],
        out_specs=vmem_spec,
        scratch_shapes=[
            vmem((D, 2 * FFL + LOW), BF16),
            vmem((FFL + LOW, D), BF16),
            vmem((NC, NY, 128, W), BF16),
            vmem((NY, 2 * NZ, 128), F32),
            vmem((NZ * PAD, NY * 128), BF16),
            vmem((NY * 128, NZ * 128), BF16),
            vmem((NC, NZ, PAD, W), BF16),
            vmem((NC, NZ, PAD, W), BF16),
            vmem((NC, 2 * NX, ALL, W), BF16),
            vmem((ALL, LOW), BF16),
            vmem((ALL, 2 * FFL + LOW), F32),
            vmem((ALL, FFL + LOW), BF16),
            vmem((NC, NX, ALL, W), BF16),
            vmem((NC, NX, ALL, W), BF16),
            vmem((NC, 3, ALL, W), BF16),
            vmem((NC, 2, HALF, W), BF16),
            vmem((NC, 2, ALL, W), BF16),
            vmem((NC, NZ, PAD, W), BF16),
            vmem((NC, NZ, 128, W), BF16),
            vmem((NC, BLOCK, W), F32),
            vmem((NC, NY, BLOCK, W), BF16),
            vmem((NC, NY, BLOCK, W), BF16),
            dma((14,)),
            dma((NC * NY,)), dma((NC * NY,)),
            dma((NY,)), dma((NY,)),
            dma((NC * NZ,)), dma((NC * NZ,)),
            dma((NC * 8,)), dma((NC * 8,)),
            dma((16,)), dma((16,)),
            dma((NC * NX,)), dma((NC * NX,)),
            dma((NC * 2,)), dma((NC * 2,)),
            dma((NC * 2,)), dma((NC * 2,)),
            dma((NC * NZ,)), dma((NC * NZ,)),
            dma((NC * NY,)), dma((NC * NY,)),
        ],
        compiler_params=pltpu.CompilerParams(
            collective_id=0, has_side_effects=True, vmem_limit_bytes=62 * 1024 * 1024
        ),
        name="moe",
    )(
        tokens, table, domhot, gate_weight[0], up_weight[0], down_weight[0],
        up_entry[0], up_exit[0], down_entry[0], down_exit[0],
    )


def solution(mesh):
    in_specs = (
        P(None, "expert", None),
        P(None, "expert", None),
        P(None, "expert", None),
        P(None, "expert"),
        P("expert", None, "dp"),
        P("expert", None, "dp"),
        P("expert", "dp", None),
        P("expert", "dp", None),
        P("expert", None, "dp"),
        P("expert", "dp", None),
        P("expert", None, "dp"),
    )
    out_specs = P(None, "expert", "dp")
    return jax.shard_map(
        on_device, mesh=mesh, in_specs=in_specs, out_specs=out_specs, check_vma=False
    )
```

```python
import jax
import jax.numpy as jnp
from jax import lax
from jax.experimental import pallas as pl
from jax.experimental.pallas import tpu as pltpu
from jax.sharding import PartitionSpec as P

MESH = pl.DeviceIdType.MESH
F32 = jnp.float32
BF16 = jnp.bfloat16

TOP = 4
RANK = 32
DOMAINS = 4
STEPS = 2
TOK = 48
CAP = 9
EXPERTS = 32
D = 7168
FFL = 256
PART = 896
LOW = RANK * DOMAINS
NX, NY, NZ = 4, 4, 8
SLOT = STEPS * CAP
ROWS = NY * SLOT
PAD = 80
ALL = NZ * ROWS
BLOCK = STEPS * TOK
W = 256
OWN = ((0, 128), (128, 128), (256, 128), (384, 128), (512, 128), (640, 128), (768, 128))
NC = len(OWN)
AWAY = (0, 2, 6, 4, 1, 7, 3, 5)
NH = 2
WIDE = max(wide for _, wide in OWN)
HALF = ALL // NH
QUART = HALF // 2

ORDER = (
    "y4", "y6", "y1", "y3", "y0", "y5", "y2", "T", "B4", "B6", "B1", "B3", "b1", "b3", "b6", "b4", "B0", "B5", "B2",
    "C4.0", "b5", "b0", "b2", "C6.0", "C1.0", "D4.0", "C3.0", "C1.1", "D6.0", "C3.1", "D1.0", "e4.0", "C6.1", "E4.0",
    "D3.0", "C4.1", "D1.1", "e6.0", "E6.0", "D3.1", "e1.0", "C0.0", "E1.0", "D6.1", "C5.0", "e3.0", "E3.0", "D4.1",
    "C2.0", "L1.0", "e3.1", "e1.1", "C5.1", "L2.0", "D0.0", "E3.1", "e6.1", "E1.1", "E6.1", "D5.0", "e4.1", "C0.1",
    "E4.1", "D2.0", "C2.1", "L1.1", "D5.1", "L2.1", "L3.0", "e0.0", "e5.0", "E0.0", "E5.0", "D0.1", "e2.0", "E2.0",
    "H.0", "D2.1", "M1.0", "P6.0", "P0.0", "M2.0", "P3.0", "Q6.0", "Q0.0", "P1.0", "Q3.0", "P4.0", "P5.0", "Q1.0",
    "P2.0", "Q4.0", "Q5.0", "L3.1", "e5.1", "Q2.0", "e2.1", "R6.0", "M3.0", "R0.0", "e0.1", "E5.1", "R3.0", "R1.0",
    "R4.0", "E0.1", "R5.0", "R2.0", "E2.1", "H.1", "S6.0", "M1.1", "P5.1", "S0.0", "M2.1", "P3.1", "S3.0", "Q5.1",
    "P2.1", "Q3.1", "S1.0", "P4.1", "Q2.1", "P1.1", "S4.0", "Q4.1", "P6.1", "S5.0", "Q1.1", "P0.1", "Q6.1", "S2.0",
    "Q0.1", "M3.1", "R5.1", "R3.1", "R2.1", "R4.1", "R1.1", "R6.1", "R0.1", "S5.1", "S3.1", "S2.1", "S4.1", "S1.1",
    "U5", "S6.1", "U3", "S0.1", "U2", "U4", "V5", "U1", "V3", "U6", "V2", "U0", "V4", "V1", "V6", "V0",
)


def dot(a, b):
    return jnp.dot(a, b, preferred_element_type=F32)


def kernel(
    tokens, facts, gate, up, down, up_enter, up_leave, down_enter, down_leave,
    out,
    ws, wd, g, table, tab, sel, selwt, zs, zr, xs, mask, acc, hid,
    lp, lq, lx, lf, sb, sr, ss, hr, tr, tp, vz, own, ys, yr,
    load_sem, tsend, trecv, ysend, yrecv, zsend, zrecv, xsend, xrecv,
    lsend, lrecv, bsend, brecv, hsend, hrecv, rsend, rrecv, vsend, vrecv, osend, orecv,
):
    dp = lax.axis_index("dp")
    ex = lax.axis_index("expert")
    x, core = dp // 2, dp % 2
    z, y = ex // NY, ex % NY
    sib = x * 2 + (1 - core)
    ip, im, io = (x + 1) % NX, (x + 3) % NX, (x + 2) % NX
    xp, xm, xo = ip * 2 + core, im * 2 + core, io * 2 + core

    def at_x(i):
        return ((x + i) % NX) * 2 + core

    def at_y(m):
        return z * NY + (y + m) % NY

    def at_z(k):
        return ((z + k) % NZ) * NY + y

    def send(src, dst, ssem, rsem, **where):
        return pltpu.make_async_remote_copy(
            src_ref=src, dst_ref=dst, send_sem=ssem, recv_sem=rsem,
            device_id=where, device_id_type=MESH,
        )

    def lanes(index, wide):
        return pl.ds(pl.multiple_of(index * wide, wide), wide)

    barrier = pltpu.get_barrier_semaphore()
    for peer in (xp, xm, xo, sib):
        pl.semaphore_signal(barrier, inc=1, device_id={"dp": peer}, device_id_type=MESH)
    for m in range(1, NY):
        pl.semaphore_signal(barrier, inc=1, device_id={"expert": at_y(m)}, device_id_type=MESH)
    for k in range(1, NZ):
        pl.semaphore_signal(barrier, inc=1, device_id={"expert": at_z(k)}, device_id_type=MESH)

    loads = []
    for c, (off, wide) in enumerate(OWN):
        for s in range(STEPS):
            loads.append(
                (
                    tokens.at[s, :, pl.ds(pl.multiple_of(dp * PART + off, 128), wide)],
                    g.at[c, 0, pl.ds(s * TOK, TOK), pl.ds(0, wide)],
                )
            )
    n_tokens = len(loads)
    for c, (off, wide) in enumerate(OWN):
        for half, array in ((0, gate), (1, up)):
            cols = pl.ds(half * FFL, FFL)
            loads.append((array.at[:, pl.ds(off, wide), :], ws[c].at[:, :, cols]))
    loads.append((down, wd))
    loads = [pltpu.make_async_copy(a, b, load_sem.at[i]) for i, (a, b) in enumerate(loads)]
    for copy in loads:
        copy.start()
    for c in range(NC):
        for m in range(NY):
            g[c, m, BLOCK:, :] = jnp.zeros((128 - BLOCK, W), BF16)
        for k in range(NZ):
            vz[c, k, PAD:, :] = jnp.zeros((128 - PAD, WIDE), BF16)
    def count(shape, dim):
        return lax.broadcasted_iota(jnp.int32, shape, dim)

    row, token = count((EXPERTS, 128), 0), count((EXPERTS, 128), 1)
    expert = ((row % NZ) * NY + row // NZ).astype(F32)
    hit, weight = jnp.zeros((EXPERTS, 128), F32), jnp.zeros((EXPERTS, 128), F32)
    for k in range(TOP):
        named = (facts[k : k + 1, :] == expert) & (token < BLOCK)
        hit += jnp.where(named, 1.0, 0.0)
        weight += jnp.where(named, facts[TOP + k : TOP + k + 1, :], 0.0)
    first, second = count((128, 128), 0), count((128, 128), 1)
    before = (first < second) & ((first >= TOK) == (second >= TOK))
    rank = dot(hit.astype(BF16), jnp.where(before, 1.0, 0.0).astype(BF16))
    code = jnp.where(hit > 0.0, rank + jnp.where(token >= TOK, float(CAP), 0.0), -1.0)
    table[:, :NZ, :] = code.reshape(NY, NZ, 128)
    table[:, NZ:, :] = weight.reshape(NY, NZ, 128)
    domain = facts[2 * TOP : 2 * TOP + 1, :] == (first // RANK).astype(F32)
    g[0, 0, :BLOCK, 128:] = jnp.where(domain, 1.0, 0.0).T[:BLOCK].astype(BF16)
    pl.semaphore_wait(barrier, 14)

    def table_copy(m):
        return send(
            table.at[(y + m) % NY], tab.at[m], tsend.at[m], trecv.at[m], expert=at_y(m)
        )

    def y_copy(c, m):
        i, cols = c * NY + m, pl.ds(0, W if c == 0 else OWN[c][1])
        return send(
            g.at[c, 0, pl.ds(0, BLOCK), cols], g.at[c, m, pl.ds(0, BLOCK), cols],
            ysend.at[i], yrecv.at[i], expert=at_y(m),
        )

    def stage_tables():
        for m in range(1, NY):
            table_copy(m).wait_recv()

        def choose(m, carry):
            for n, k in enumerate(AWAY):
                zd = (z + k) % NZ
                code, weight = tab[m, pl.ds(zd, 1), :], tab[m, pl.ds(NZ + zd, 1), :]
                code = jnp.where(code >= 0.0, code + (m * SLOT).astype(F32), -1.0)
                at = lax.broadcasted_iota(jnp.int32, (128, 128), 0).astype(F32) == code
                hot = jnp.where(at, 1.0, 0.0)[:PAD].astype(BF16)
                cols = pl.ds(pl.multiple_of(m * 128, 128), 128)
                sel[n * PAD : (n + 1) * PAD, cols] = hot
                selwt[cols, n * 128 : (n + 1) * 128] = jnp.where(at, weight, 0.0).T.astype(BF16)
            return carry

        lax.fori_loop(0, NY, choose, 0)

    def z_copy(c, n):
        i = c * NZ + n
        cols = pl.ds(0, W if c == 0 else OWN[c][1])
        return send(
            zs.at[c, n, :, cols], zr.at[c, n, :, cols], zsend.at[i], zrecv.at[i],
            expert=at_z(AWAY[n]),
        )

    def of_half(h):
        return [n for n in range(4 * h, 4 * h + 4) if n > 0]

    def stage_y(c):
        for copy in loads[c * STEPS : (c + 1) * STEPS]:
            copy.wait()
        for m in range(1, NY):
            y_copy(c, m).start()

    def stage_b(c):
        for m in range(1, NY):
            y_copy(c, m).wait_recv()
        take = W if c == 0 else OWN[c][1]
        rows = dot(sel[...], g[c, :, :, :take].reshape(NY * 128, take))
        rows = rows.astype(BF16).reshape(NZ, PAD, take)
        zs[c, :, :, :take] = rows
        for n in of_half(0):
            z_copy(c, n).start()
        zr[c, 0, :, :take] = rows[0]

    def stage_b2(c):
        for n in of_half(1):
            z_copy(c, n).start()

    def near(c, h, kind, to, who):
        n = (c * NH + h) * 8 + kind
        block = xs[c].at[pl.ds(h * HALF, HALF), lanes(who, OWN[c][1])]
        return send(block, block, xsend.at[n], xrecv.at[n], dp=to)

    def far(c, h, kind, to, who):
        n = (c * NH + h) * 8 + kind
        block = xs[c].at[pl.ds(h * HALF + (kind - 3) * QUART, QUART), lanes(who, OWN[c][1])]
        return send(block, block, xsend.at[n], xrecv.at[n], dp=to)

    def stage_c(c, h):
        for n in of_half(h):
            z_copy(c, n).wait_recv()
        wide, mine = OWN[c][1], slice(h * HALF, (h + 1) * HALF)
        take = W if c == 0 else wide
        rows = zr[c, 4 * h : 4 * h + 4, :, :take].astype(F32)[:, :ROWS]
        rows = rows.reshape(HALF, take).astype(BF16)
        xs[c][mine, lanes(dp, wide)] = rows[:, :wide]
        if c == 0:
            mask[mine, :] = rows[:, 128:]
        near(c, h, 0, xp, dp).start()
        near(c, h, 1, xm, dp).start()
        near(c, h, 2, sib, dp).start()

    def stage_d(c, h):
        near(c, h, 0, xp, xm).wait_recv()
        far(c, h, 3, xp, xm).start()
        near(c, h, 5, sib, xm).start()
        near(c, h, 1, xm, xp).wait_recv()
        far(c, h, 4, xm, xp).start()
        near(c, h, 6, sib, xp).start()

    started = [False] * NH

    def stage_e(c, h):
        far(c, h, 3, xp, xo).wait_recv()
        far(c, h, 4, xm, xo).wait_recv()
        near(c, h, 7, sib, xo).start()

    loaded = set()

    def stage_e2(c, h):
        for kind, step in ((2, 0), (5, 3), (6, 1), (7, 2)):
            near(c, h, kind, sib, ((x + step) % NX) * 2 + 1 - core).wait_recv()
        if c not in loaded:
            loaded.add(c)
            for half in range(2):
                loads[n_tokens + c * 2 + half].wait()
        mine, wide = slice(h * HALF, (h + 1) * HALF), OWN[c][1]
        term = dot(xs[c][mine, :], ws[c][...].reshape(8 * wide, 2 * FFL))
        if started[h]:
            acc[mine, :] += term
        else:
            acc[mine, :] = term
            started[h] = True

    def pair_copy(q, h):
        n = (q * NH + h) * 8
        away = pl.ds(pl.multiple_of(h * HALF + (1 - core) * QUART, 16), QUART)
        return send(lp.at[q, away], lq.at[q, h], lsend.at[n], lrecv.at[n], dp=sib)

    def low_copy(q, h, j):
        n = (q * NH + h) * 8 + j
        return send(lx.at[q, h, 0], lx.at[q, h, j], lsend.at[n], lrecv.at[n], dp=at_x(j))

    def back_copy(q, h, whose):
        n = (q * NH + h) * 8 + 4
        rows = lf.at[q, pl.ds(pl.multiple_of(h * HALF + whose * QUART, 16), QUART)]
        return send(rows, rows, lsend.at[n], lrecv.at[n], dp=sib)

    def stage_low(s, q, h):
        mine = slice(h * HALF, (h + 1) * HALF)
        home = pl.ds(pl.multiple_of(h * HALF + core * QUART, 16), QUART)
        if s == 1:
            if q == 0:
                total = jnp.zeros((HALF, LOW), F32)
                for c, (off, wide) in enumerate(OWN):
                    block = xs[c][mine, lanes(dp, wide)]
                    total += dot(block, up_enter[off : off + wide, :])
            else:
                total = dot(hid[mine, :], down_enter[...])
            lp[q, mine, :] = total.astype(BF16)
            pair_copy(q, h).start()
        elif s == 2:
            pair_copy(q, h).wait_recv()
            lx[q, h, 0] = (lp[q, home, :].astype(F32) + lq[q, h].astype(F32)).astype(BF16)
            for j in range(1, NX):
                low_copy(q, h, j).start()
        elif s == 3:
            total = lx[q, h, 0].astype(F32)
            for j in range(1, NX):
                low_copy(q, h, j).wait_recv()
                total += lx[q, h, j].astype(F32)
            lf[q, home, :] = (total * mask[home, :].astype(F32)).astype(BF16)
            back_copy(q, h, core).start()

    def stage_hidden(h):
        mine = slice(h * HALF, (h + 1) * HALF)
        back_copy(0, h, 1 - core).wait_recv()
        gated = acc[mine, :FFL]
        upped = acc[mine, FFL:] + dot(lf[0, mine, :], up_leave[...])
        hid[mine, :] = (gated / (1.0 + jnp.exp(-gated)) * upped).astype(BF16)
        if "down" not in loaded:
            loaded.add("down")
            loads[-1].wait()

    def partial(c, h, shard):
        off, wide = OWN[c]
        cols = pl.ds(pl.multiple_of(shard * PART + off, 128), wide)
        return dot(hid[h * HALF : (h + 1) * HALF, :], wd[:, cols])

    def b_copy(c, h, i):
        cols, n = pl.ds(0, OWN[c][1]), (c * NH + h) * NX + i
        rows = pl.ds(h * HALF, HALF)
        return send(
            sb.at[c, i, rows, cols], sr.at[c, i, rows, cols], bsend.at[n], brecv.at[n], dp=sib
        )

    def paired(c, h, i):
        b_copy(c, h, i).wait_recv()
        more = sr[c, i, h * HALF : (h + 1) * HALF, : OWN[c][1]].astype(F32)
        return partial(c, h, i * 2 + core) + more

    def h_copy(c, h, i):
        cols, n = pl.ds(0, OWN[c][1]), (c * NH + h) * 2 + i
        return send(
            ss.at[c, h, 2, pl.ds(i * QUART, QUART), cols], hr.at[c, h, i, :, cols],
            hsend.at[n], hrecv.at[n], dp=(xp, xm)[i],
        )

    def r_copy(c, h, i):
        cols, n = pl.ds(0, OWN[c][1]), (c * NH + h) * 2 + i
        return send(
            ss.at[c, h, i, :, cols], tr.at[c, h, i, :, cols],
            rsend.at[n], rrecv.at[n], dp=(xp, xm)[i],
        )

    def v_copy(c, n):
        cols, i = pl.ds(0, OWN[c][1]), c * NZ + n
        return send(
            tp.at[c, n, :, cols], vz.at[c, n, pl.ds(0, PAD), cols],
            vsend.at[i], vrecv.at[i], expert=at_z(NZ - AWAY[n]),
        )

    def o_copy(c, m):
        cols, n = pl.ds(0, OWN[c][1]), c * NY + m
        return send(
            ys.at[c, m, :, cols], yr.at[c, m, :, cols], osend.at[n], orecv.at[n],
            expert=at_y(NY - m),
        )

    def stage_1(c, h):
        wide = OWN[c][1]

        def one(j, carry):
            i = (x + 2 + j) % NX
            term = partial(c, h, i * 2 + 1 - core)
            sb[c, i, h * HALF : (h + 1) * HALF, :wide] = term.astype(BF16)
            b_copy(c, h, i).start()
            return carry

        lax.fori_loop(0, NX, one, 0)

    def stage_2(c, h):
        ss[c, h, 2, :, : OWN[c][1]] = paired(c, h, io).astype(BF16)
        h_copy(c, h, 0).start()
        h_copy(c, h, 1).start()

    def stage_3(c, h):
        wide = OWN[c][1]
        for i, to in enumerate((ip, im)):
            total = paired(c, h, to)
            h_copy(c, h, i).wait_recv()
            more = hr[c, h, i, :, :wide].astype(F32)
            if i == 0:
                ss[c, h, 0, :QUART, :wide] = (total[:QUART] + more).astype(BF16)
                ss[c, h, 0, QUART:, :wide] = total[QUART:].astype(BF16)
            else:
                ss[c, h, 1, :QUART, :wide] = total[:QUART].astype(BF16)
                ss[c, h, 1, QUART:, :wide] = (total[QUART:] + more).astype(BF16)
            r_copy(c, h, i).start()

    def stage_4(c, h):
        off, wide = OWN[c]
        if ("low", h) not in loaded:
            loaded.add(("low", h))
            back_copy(1, h, 1 - core).wait_recv()
        total = paired(c, h, x)
        total += dot(lf[1, h * HALF : (h + 1) * HALF, :], down_leave[:, off : off + wide])
        for i in range(2):
            r_copy(c, h, i).wait_recv()
            total += tr[c, h, i, :, :wide].astype(F32)
        total = total.reshape(4, ROWS, wide)
        total = jnp.concatenate([total, jnp.zeros((4, PAD - ROWS, wide), F32)], axis=1)
        rows = total.astype(BF16)
        tp[c, 4 * h : 4 * h + 4, :, :wide] = rows
        for n in of_half(h):
            v_copy(c, n).start()
        if h == 0:
            vz[c, 0, :PAD, :wide] = rows[0]

    def stage_5(c):
        wide = OWN[c][1]
        for n in range(1, NZ):
            v_copy(c, n).wait_recv()
        rows = vz[c, :, :, :wide].reshape(NZ * 128, wide)
        mixed = dot(selwt[...], rows).reshape(NY, 128, wide)[:, :BLOCK]
        for m in range(1, NY):
            ys[c, m, :, :wide] = mixed[m].astype(BF16)
            o_copy(c, m).start()
        own[c, :, :wide] = mixed[0]

    def stage_6(c):
        off, wide = OWN[c]
        total = own[c, :, :wide]
        for m in range(1, NY):
            o_copy(c, m).wait_recv()
            total += yr[c, m, :, :wide].astype(F32)
        total = total.astype(BF16)
        for s in range(STEPS):
            out[s, :, off : off + wide] = total[s * TOK : (s + 1) * TOK]

    for m in range(1, NY):
        table_copy(m).start()
    tab[0] = table[y]
    stages = {
        "T": stage_tables, "y": stage_y, "B": stage_b, "b": stage_b2, "C": stage_c, "D": stage_d,
        "e": stage_e, "E": stage_e2, "H": stage_hidden, "P": stage_1, "Q": stage_2, "R": stage_3,
        "S": stage_4, "U": stage_5, "V": stage_6,
    }
    def sent_out(c):
        for m in range(1, NY):
            y_copy(c, m).wait_send()
        for n in range(1, NZ):
            z_copy(c, n).wait_send()
        for h in range(NH):
            for kind in (0, 1, 2, 5, 6, 7):
                near(c, h, kind, sib, dp).wait_send()
            for i in range(2):
                far(c, h, 3 + i, xp, dp).wait_send()

    def sent_back():
        for m in range(1, NY):
            table_copy(m).wait_send()
        for h in range(NH):
            for q in range(2):
                pair_copy(q, h).wait_send()
                back_copy(q, h, core).wait_send()
                for j in range(1, NX):
                    low_copy(q, h, j).wait_send()
            for c in range(NC):
                for i in range(2):
                    h_copy(c, h, i).wait_send()
                    r_copy(c, h, i).wait_send()
                for i in range(NX):
                    b_copy(c, h, i).wait_send()
        for c in range(NC):
            for n in range(1, NZ):
                v_copy(c, n).wait_send()

    mixes = 0
    for name in ORDER:
        if name[0] == "U":
            sent_out(mixes)
            mixes += 1
            if mixes == NC:
                sent_back()
        numbers = [int(n) for n in name[1:].split(".") if n]
        if name[0] in "LM":
            stage_low(numbers[0], "LM".index(name[0]), numbers[1])
        else:
            stages[name[0]](*numbers)

    for c in range(NC):
        for m in range(1, NY):
            o_copy(c, m).wait_send()


def on_device(
    tokens,
    routes,
    route_weights,
    domains,
    gate_weight,
    up_weight,
    down_weight,
    up_entry,
    up_exit,
    down_entry,
    down_exit,
):
    facts = jnp.concatenate(
        [
            jnp.transpose(routes.reshape(BLOCK, TOP)).astype(F32),
            jnp.transpose(route_weights.reshape(BLOCK, TOP)),
            domains.reshape(1, BLOCK).astype(F32),
        ]
    )
    facts = jnp.pad(facts, ((0, 16 - 2 * TOP - 1), (0, 128 - BLOCK)))

    any_spec = pl.BlockSpec(memory_space=pl.ANY)
    vmem_spec = pl.BlockSpec(memory_space=pltpu.VMEM)
    dma = pltpu.SemaphoreType.DMA
    vmem = pltpu.VMEM
    return pl.pallas_call(
        kernel,
        out_shape=jax.ShapeDtypeStruct((STEPS, TOK, PART), BF16),
        in_specs=[any_spec, vmem_spec] + [any_spec] * 3 + [vmem_spec] * 4,
        out_specs=vmem_spec,
        scratch_shapes=[
            [vmem((8, wide, 2 * FFL), BF16) for _, wide in OWN],
            vmem((FFL, D), BF16),
            vmem((NC, NY, 128, W), BF16),
            vmem((NY, 2 * NZ, 128), F32),
            vmem((NY, 2 * NZ, 128), F32),
            vmem((NZ * PAD, NY * 128), BF16),
            vmem((NY * 128, NZ * 128), BF16),
            vmem((NC, NZ, PAD, W), BF16),
            vmem((NC, NZ, PAD, W), BF16),
            [vmem((ALL, 8 * wide), BF16) for _, wide in OWN],
            vmem((ALL, LOW), BF16),
            vmem((ALL, 2 * FFL), F32),
            vmem((ALL, FFL), BF16),
            vmem((2, ALL, LOW), BF16),
            vmem((2, NH, QUART, LOW), BF16),
            vmem((2, NH, NX, QUART, LOW), BF16),
            vmem((2, ALL, LOW), BF16),
            vmem((NC, NX, ALL, WIDE), BF16),
            vmem((NC, NX, ALL, WIDE), BF16),
            vmem((NC, NH, 3, HALF, WIDE), BF16),
            vmem((NC, NH, 2, QUART, WIDE), BF16),
            vmem((NC, NH, 2, HALF, WIDE), BF16),
            vmem((NC, NZ, PAD, WIDE), BF16),
            vmem((NC, NZ, 128, WIDE), BF16),
            vmem((NC, BLOCK, WIDE), F32),
            vmem((NC, NY, BLOCK, WIDE), BF16),
            vmem((NC, NY, BLOCK, WIDE), BF16),
            dma((4 * NC + 1,)),
            dma((NY,)), dma((NY,)),
            dma((NC * NY,)), dma((NC * NY,)),
            dma((NC * NZ,)), dma((NC * NZ,)),
            dma((NC * NH * 8,)), dma((NC * NH * 8,)),
            dma((NH * 16,)), dma((NH * 16,)),
            dma((NC * NH * NX,)), dma((NC * NH * NX,)),
            dma((NC * NH * 2,)), dma((NC * NH * 2,)),
            dma((NC * NH * 2,)), dma((NC * NH * 2,)),
            dma((NC * NZ,)), dma((NC * NZ,)),
            dma((NC * NY,)), dma((NC * NY,)),
        ],
        compiler_params=pltpu.CompilerParams(
            collective_id=0, has_side_effects=True, vmem_limit_bytes=62 * 1024 * 1024
        ),
        name="moe",
    )(
        tokens, facts,
        gate_weight[0].reshape(8, PART, FFL), up_weight[0].reshape(8, PART, FFL), down_weight[0],
        up_entry[0], up_exit[0], down_entry[0], down_exit[0],
    )


def solution(mesh):
    in_specs = (
        P(None, "expert", None),
        P(None, "expert", None),
        P(None, "expert", None),
        P(None, "expert"),
        P("expert", None, "dp"),
        P("expert", None, "dp"),
        P("expert", "dp", None),
        P("expert", "dp", None),
        P("expert", None, "dp"),
        P("expert", "dp", None),
        P("expert", None, "dp"),
    )
    out_specs = P(None, "expert", "dp")
    return jax.shard_map(
        on_device, mesh=mesh, in_specs=in_specs, out_specs=out_specs, check_vma=False
    )
```

```python
import jax
import jax.numpy as jnp
from jax import lax
from jax.experimental import pallas as pl
from jax.experimental.pallas import tpu as pltpu
from jax.sharding import PartitionSpec as P

MESH = pl.DeviceIdType.MESH
F32 = jnp.float32
BF16 = jnp.bfloat16

TOP = 4
RANK = 32
DOMAINS = 4
STEPS = 2
TOK = 48
CAP = 9
EXPERTS = 32
D = 7168
FFL = 256
PART = 896
LOW = RANK * DOMAINS
NX, NY, NZ = 4, 4, 8
SLOT = STEPS * CAP
ROWS = NY * SLOT
PAD = 80
ALL = NZ * ROWS
BLOCK = STEPS * TOK
W = 256
OWN = ((0, 128), (128, 128), (256, 128), (384, 128), (512, 128), (640, 128), (768, 128))
NC = len(OWN)
AWAY = (0, 2, 6, 4, 1, 7, 3, 5)
NH = 2
WIDE = max(wide for _, wide in OWN)
HALF = ALL // NH
QUART = HALF // 2

ORDER = (
    "y0", "y1", "y2", "y3", "y4", "y5", "G1", "y6", "T", "B0", "B1", "B2", "b0", "B3", "G2", "B4", "B5", "B6", "b1",
    "b2", "b3", "b4", "b5", "b6", "C0.0", "G3", "C1.0", "C2.0", "D0.0", "C0.1", "D1.0", "D2.0", "C3.0", "e0.0",
    "C4.0", "E0.0", "D0.1", "e1.0", "C5.0", "e2.0", "E1.0", "C6.0", "D3.0", "E2.0", "C1.1", "D4.0", "C2.1", "e0.1",
    "D5.0", "C3.1", "E0.1", "D6.0", "C4.1", "e3.0", "C5.1", "D1.1", "E3.0", "e4.0", "C6.1", "D2.1", "E4.0", "e5.0",
    "E5.0", "D3.1", "e6.0", "E6.0", "D4.1", "H.0", "M1.0", "D5.1", "P1.0", "M2.0", "P5.0", "P6.0", "D6.1", "Q1.0",
    "Q5.0", "P4.0", "Q6.0", "P2.0", "P0.0", "Q4.0", "P3.0", "Q2.0", "Q0.0", "e1.1", "e2.1", "Q3.0", "e3.1", "e4.1",
    "E1.1", "M3.0", "R1.0", "E2.1", "R5.0", "R6.0", "E3.1", "R4.0", "R2.0", "e5.1", "R0.0", "E4.1", "R3.0", "e6.1",
    "E5.1", "S1.0", "E6.1", "H.1", "M1.1", "S5.0", "P1.1", "M2.1", "S6.0", "P5.1", "S4.0", "Q1.1", "P6.1", "S2.0",
    "Q5.1", "P4.1", "Q6.1", "S0.0", "P2.1", "Q4.1", "P0.1", "S3.0", "Q2.1", "P3.1", "Q0.1", "M3.1", "R1.1", "Q3.1",
    "R5.1", "R6.1", "R4.1", "R2.1", "R0.1", "S1.1", "R3.1", "S5.1", "S6.1", "S4.1", "S2.1", "U1", "S0.1", "S3.1",
    "U5", "U6", "U4", "V1", "U2", "U0", "V5", "U3", "V6", "V4", "V2", "V0", "V3",
)


def dot(a, b):
    return jnp.dot(a, b, preferred_element_type=F32)


def kernel(
    tokens, routes, route_weights, domains, gate, up, down, up_enter, up_leave, down_enter, down_leave,
    out,
    ws, ent, wd, g, raw, table, tab, sel, selwt, zs, zr, xs, mask, acc, accl, hid,
    lp, lq, lx, lf, sb, sr, ss, hr, tr, tp, vz, own, ys, yr,
    load_sem, esend, erecv, tsend, trecv, ysend, yrecv, zsend, zrecv, xsend, xrecv,
    lsend, lrecv, bsend, brecv, hsend, hrecv, rsend, rrecv, vsend, vrecv, osend, orecv,
):
    dp = lax.axis_index("dp")
    ex = lax.axis_index("expert")
    x, core = dp // 2, dp % 2
    z, y = ex // NY, ex % NY
    sib = x * 2 + (1 - core)
    ip, im, io = (x + 1) % NX, (x + 3) % NX, (x + 2) % NX
    xp, xm, xo = ip * 2 + core, im * 2 + core, io * 2 + core

    def at_x(i):
        return ((x + i) % NX) * 2 + core

    def at_y(m):
        return z * NY + (y + m) % NY

    def at_z(k):
        return ((z + k) % NZ) * NY + y

    def send(src, dst, ssem, rsem, **where):
        return pltpu.make_async_remote_copy(
            src_ref=src, dst_ref=dst, send_sem=ssem, recv_sem=rsem,
            device_id=where, device_id_type=MESH,
        )

    def lanes(index, wide):
        return pl.ds(pl.multiple_of(index * wide, wide), wide)

    barrier = pltpu.get_barrier_semaphore()
    for peer in (xp, xm, xo, sib):
        pl.semaphore_signal(barrier, inc=1, device_id={"dp": peer}, device_id_type=MESH)
    for m in range(1, NY):
        pl.semaphore_signal(barrier, inc=1, device_id={"expert": at_y(m)}, device_id_type=MESH)
    for k in range(1, NZ):
        pl.semaphore_signal(barrier, inc=1, device_id={"expert": at_z(k)}, device_id_type=MESH)

    loads = []
    for c, (off, wide) in enumerate(OWN):
        for s in range(STEPS):
            loads.append(
                (
                    tokens.at[s, :, pl.ds(pl.multiple_of(dp * PART + off, 128), wide)],
                    g.at[c, 0, pl.ds(s * TOK, TOK), pl.ds(0, wide)],
                )
            )
    n_tokens = len(loads)
    for c, (off, wide) in enumerate(OWN):
        for half, array in ((0, gate), (1, up)):
            cols = pl.ds(half * FFL, FFL)
            for side in range(2):
                rows = array.at[:, side, pl.ds(off, wide), :]
                loads.append((rows, ws[c].at[pl.ds(side * NX, NX), :, cols]))
    loads.append((down, wd))
    loads = [pltpu.make_async_copy(a, b, load_sem.at[i]) for i, (a, b) in enumerate(loads)]
    enter_load = pltpu.make_async_copy(up_enter, ent.at[core * NX + x], load_sem.at[len(loads)])
    for copy in loads[:n_tokens] + [enter_load] + loads[n_tokens:]:
        copy.start()
    for c in range(NC):
        for m in range(NY):
            g[c, m, BLOCK:, :] = jnp.zeros((128 - BLOCK, W), BF16)
        for k in range(NZ):
            vz[c, k, PAD:, :] = jnp.zeros((128 - PAD, WIDE), BF16)
    def count(shape, dim):
        return lax.broadcasted_iota(jnp.int32, shape, dim)

    raw[...] = jnp.zeros_like(raw)
    for s in range(STEPS):
        raw[s * TOK : (s + 1) * TOK, :TOP] = routes[s].astype(F32)
        raw[s * TOK : (s + 1) * TOK, TOP : 2 * TOP] = route_weights[s]
    facts = raw[...].T
    of_token = jnp.concatenate([domains[s : s + 1, :].astype(F32) for s in range(STEPS)], axis=1)
    row, token = count((EXPERTS, 128), 0), count((EXPERTS, 128), 1)
    expert = ((row % NZ) * NY + row // NZ).astype(F32)
    hit, weight = jnp.zeros((EXPERTS, 128), F32), jnp.zeros((EXPERTS, 128), F32)
    for k in range(TOP):
        named = (facts[k : k + 1, :] == expert) & (token < BLOCK)
        hit += jnp.where(named, 1.0, 0.0)
        weight += jnp.where(named, facts[TOP + k : TOP + k + 1, :], 0.0)
    first, second = count((128, 128), 0), count((128, 128), 1)
    before = (first < second) & ((first >= TOK) == (second >= TOK))
    rank = dot(hit.astype(BF16), jnp.where(before, 1.0, 0.0).astype(BF16))
    code = jnp.where(hit > 0.0, rank + jnp.where(token >= TOK, float(CAP), 0.0), -1.0)
    table[:, :NZ, :] = code.reshape(NY, NZ, 128)
    table[:, NZ:, :] = weight.reshape(NY, NZ, 128)
    of_token = jnp.concatenate([of_token, jnp.zeros((1, 128 - BLOCK), F32)], axis=1)
    domain = of_token == (first // RANK).astype(F32)
    g[0, 0, :BLOCK, 128:] = jnp.where(domain, 1.0, 0.0).T[:BLOCK].astype(BF16)
    pl.semaphore_wait(barrier, 14)

    def table_copy(m):
        return send(
            table.at[(y + m) % NY], tab.at[m], tsend.at[m], trecv.at[m], expert=at_y(m)
        )

    def y_copy(c, m):
        i, cols = c * NY + m, pl.ds(0, W if c == 0 else OWN[c][1])
        return send(
            g.at[c, 0, pl.ds(0, BLOCK), cols], g.at[c, m, pl.ds(0, BLOCK), cols],
            ysend.at[i], yrecv.at[i], expert=at_y(m),
        )

    def stage_tables():
        for m in range(1, NY):
            table_copy(m).wait_recv()

        def choose(m, carry):
            for n, k in enumerate(AWAY):
                zd = (z + k) % NZ
                code, weight = tab[m, pl.ds(zd, 1), :], tab[m, pl.ds(NZ + zd, 1), :]
                code = jnp.where(code >= 0.0, code + (m * SLOT).astype(F32), -1.0)
                at = lax.broadcasted_iota(jnp.int32, (128, 128), 0).astype(F32) == code
                hot = jnp.where(at, 1.0, 0.0)[:PAD].astype(BF16)
                cols = pl.ds(pl.multiple_of(m * 128, 128), 128)
                sel[n * PAD : (n + 1) * PAD, cols] = hot
                selwt[cols, n * 128 : (n + 1) * 128] = jnp.where(at, weight, 0.0).T.astype(BF16)
            return carry

        lax.fori_loop(0, NY, choose, 0)

    def z_copy(c, n):
        i = c * NZ + n
        cols = pl.ds(0, W if c == 0 else OWN[c][1])
        return send(
            zs.at[c, n, :, cols], zr.at[c, n, :, cols], zsend.at[i], zrecv.at[i],
            expert=at_z(AWAY[n]),
        )

    def of_half(h):
        return [n for n in range(4 * h, 4 * h + 4) if n > 0]

    def stage_y(c):
        for copy in loads[c * STEPS : (c + 1) * STEPS]:
            copy.wait()
        for m in range(1, NY):
            y_copy(c, m).start()

    def stage_b(c):
        for m in range(1, NY):
            y_copy(c, m).wait_recv()
        take = W if c == 0 else OWN[c][1]
        rows = dot(sel[...], g[c, :, :, :take].reshape(NY * 128, take))
        rows = rows.astype(BF16).reshape(NZ, PAD, take)
        zs[c, :, :, :take] = rows
        for n in of_half(0):
            z_copy(c, n).start()
        zr[c, 0, :, :take] = rows[0]

    def stage_b2(c):
        for n in of_half(1):
            z_copy(c, n).start()

    def near(c, h, kind, to, whose):
        n = (c * NH + h) * 5 + kind
        block = xs[c].at[pl.ds(h * HALF, HALF), lanes(core * NX + whose, OWN[c][1])]
        return send(block, block, xsend.at[n], xrecv.at[n], dp=to)

    def far(c, h, kind, to, whose):
        n = (c * NH + h) * 5 + kind
        rows = pl.ds(h * HALF + (kind - 2) * QUART, QUART)
        block = xs[c].at[rows, lanes(core * NX + whose, OWN[c][1])]
        return send(block, block, xsend.at[n], xrecv.at[n], dp=to)

    def cross(c, h, side):
        n = (c * NH + h) * 5 + 4
        block = xs[c].at[pl.ds(h * HALF, HALF), lanes(side, NX * OWN[c][1])]
        return send(block, block, xsend.at[n], xrecv.at[n], dp=sib)

    def stage_c(c, h):
        for n in of_half(h):
            z_copy(c, n).wait_recv()
        wide, mine = OWN[c][1], slice(h * HALF, (h + 1) * HALF)
        take = W if c == 0 else wide
        rows = zr[c, 4 * h : 4 * h + 4, :, :take].astype(F32)[:, :ROWS]
        rows = rows.reshape(HALF, take).astype(BF16)
        xs[c][mine, lanes(core * NX + x, wide)] = rows[:, :wide]
        if c == 0:
            mask[mine, :] = rows[:, 128:]
        near(c, h, 0, xp, x).start()
        near(c, h, 1, xm, x).start()

    def stage_d(c, h):
        near(c, h, 0, xp, im).wait_recv()
        far(c, h, 2, xp, im).start()
        near(c, h, 1, xm, ip).wait_recv()
        far(c, h, 3, xm, ip).start()

    started = [False] * NH

    def stage_e(c, h):
        far(c, h, 2, xp, io).wait_recv()
        far(c, h, 3, xm, io).wait_recv()
        cross(c, h, core).start()

    loaded = set()

    def enter_copy(kind, to, whose):
        rows = pl.ds(0, PART) if kind < 2 else pl.ds((kind - 2) * (PART // 2), PART // 2)
        block = ent.at[core * NX + whose, rows]
        return send(block, block, esend.at[kind], erecv.at[kind], dp=to)

    def enter_cross(side):
        block = ent.at[pl.ds(side * NX, NX)]
        return send(block, block, esend.at[4], erecv.at[4], dp=sib)

    def stage_g(s):
        if s == 1:
            enter_load.wait()
            enter_copy(0, xp, x).start()
            enter_copy(1, xm, x).start()
        elif s == 2:
            enter_copy(0, xp, im).wait_recv()
            enter_copy(2, xp, im).start()
            enter_copy(1, xm, ip).wait_recv()
            enter_copy(3, xm, ip).start()
        else:
            enter_copy(2, xp, io).wait_recv()
            enter_copy(3, xm, io).wait_recv()
            enter_cross(core).start()

    def stage_e2(c, h):
        cross(c, h, 1 - core).wait_recv()
        if "enter" not in loaded:
            loaded.add("enter")
            enter_cross(1 - core).wait_recv()
        if c not in loaded:
            loaded.add(c)
            for n in range(4):
                loads[n_tokens + c * 4 + n].wait()
        mine, wide = slice(h * HALF, (h + 1) * HALF), OWN[c][1]
        term = dot(xs[c][mine, :], ws[c][...].reshape(8 * wide, 2 * FFL))
        off = OWN[c][0]
        low = dot(xs[c][mine, :], ent[:, off : off + wide, :].reshape(8 * wide, LOW))
        if started[h]:
            acc[mine, :] += term
            accl[mine, :] += low
        else:
            acc[mine, :] = term
            accl[mine, :] = low
            started[h] = True

    def pair_copy(q, h):
        n = (q * NH + h) * 8
        away = pl.ds(pl.multiple_of(h * HALF + (1 - core) * QUART, 16), QUART)
        return send(lp.at[q, away], lq.at[q, h], lsend.at[n], lrecv.at[n], dp=sib)

    def low_copy(q, h, j):
        n = (q * NH + h) * 8 + j
        return send(lx.at[q, h, 0], lx.at[q, h, j], lsend.at[n], lrecv.at[n], dp=at_x(j))

    def back_copy(q, h, whose):
        n = (q * NH + h) * 8 + 4
        rows = lf.at[q, pl.ds(pl.multiple_of(h * HALF + whose * QUART, 16), QUART)]
        return send(rows, rows, lsend.at[n], lrecv.at[n], dp=sib)

    def stage_low(s, q, h):
        mine = slice(h * HALF, (h + 1) * HALF)
        home = pl.ds(pl.multiple_of(h * HALF + core * QUART, 16), QUART)
        if s == 1:
            total = dot(hid[mine, :], down_enter[...])
            lp[q, mine, :] = total.astype(BF16)
            pair_copy(q, h).start()
        elif s == 2:
            pair_copy(q, h).wait_recv()
            lx[q, h, 0] = (lp[q, home, :].astype(F32) + lq[q, h].astype(F32)).astype(BF16)
            for j in range(1, NX):
                low_copy(q, h, j).start()
        elif s == 3:
            total = lx[q, h, 0].astype(F32)
            for j in range(1, NX):
                low_copy(q, h, j).wait_recv()
                total += lx[q, h, j].astype(F32)
            lf[q, home, :] = (total * mask[home, :].astype(F32)).astype(BF16)
            back_copy(q, h, core).start()

    def stage_hidden(h):
        mine = slice(h * HALF, (h + 1) * HALF)
        gated = acc[mine, :FFL]
        low = (accl[mine, :] * mask[mine, :].astype(F32)).astype(BF16)
        upped = acc[mine, FFL:] + dot(low, up_leave[...])
        hid[mine, :] = (gated / (1.0 + jnp.exp(-gated)) * upped).astype(BF16)
        if "down" not in loaded:
            loaded.add("down")
            loads[-1].wait()

    def partial(c, h, shard):
        off, wide = OWN[c]
        cols = pl.ds(pl.multiple_of(shard * PART + off, 128), wide)
        return dot(hid[h * HALF : (h + 1) * HALF, :], wd[:, cols])

    def b_copy(c, h):
        cols, n = pl.ds(0, OWN[c][1]), c * NH + h
        rows = pl.ds(h * HALF, HALF)
        return send(
            sb.at[c, :, rows, cols], sr.at[c, :, rows, cols], bsend.at[n], brecv.at[n], dp=sib
        )

    def paired(c, h, i):
        more = sr[c, i, h * HALF : (h + 1) * HALF, : OWN[c][1]].astype(F32)
        return partial(c, h, i * 2 + core) + more

    def h_copy(c, h, i):
        cols, n = pl.ds(0, OWN[c][1]), (c * NH + h) * 2 + i
        return send(
            ss.at[c, h, 2, pl.ds(i * QUART, QUART), cols], hr.at[c, h, i, :, cols],
            hsend.at[n], hrecv.at[n], dp=(xp, xm)[i],
        )

    def r_copy(c, h, i):
        cols, n = pl.ds(0, OWN[c][1]), (c * NH + h) * 2 + i
        return send(
            ss.at[c, h, i, :, cols], tr.at[c, h, i, :, cols],
            rsend.at[n], rrecv.at[n], dp=(xp, xm)[i],
        )

    def v_copy(c, n):
        cols, i = pl.ds(0, OWN[c][1]), c * NZ + n
        return send(
            tp.at[c, n, :, cols], vz.at[c, n, pl.ds(0, PAD), cols],
            vsend.at[i], vrecv.at[i], expert=at_z(NZ - AWAY[n]),
        )

    def o_copy(c, m):
        cols, n = pl.ds(0, OWN[c][1]), c * NY + m
        return send(
            ys.at[c, m, :, cols], yr.at[c, m, :, cols], osend.at[n], orecv.at[n],
            expert=at_y(NY - m),
        )

    def stage_1(c, h):
        wide = OWN[c][1]

        def one(i, carry):
            term = partial(c, h, i * 2 + 1 - core)
            sb[c, i, h * HALF : (h + 1) * HALF, :wide] = term.astype(BF16)
            return carry

        lax.fori_loop(0, NX, one, 0)
        b_copy(c, h).start()

    def stage_2(c, h):
        b_copy(c, h).wait_recv()
        ss[c, h, 2, :, : OWN[c][1]] = paired(c, h, io).astype(BF16)
        h_copy(c, h, 0).start()
        h_copy(c, h, 1).start()

    def stage_3(c, h):
        wide = OWN[c][1]
        for i, to in enumerate((ip, im)):
            total = paired(c, h, to)
            h_copy(c, h, i).wait_recv()
            more = hr[c, h, i, :, :wide].astype(F32)
            if i == 0:
                ss[c, h, 0, :QUART, :wide] = (total[:QUART] + more).astype(BF16)
                ss[c, h, 0, QUART:, :wide] = total[QUART:].astype(BF16)
            else:
                ss[c, h, 1, :QUART, :wide] = total[:QUART].astype(BF16)
                ss[c, h, 1, QUART:, :wide] = (total[QUART:] + more).astype(BF16)
            r_copy(c, h, i).start()

    def stage_4(c, h):
        off, wide = OWN[c]
        if ("low", h) not in loaded:
            loaded.add(("low", h))
            back_copy(0, h, 1 - core).wait_recv()
        total = paired(c, h, x)
        total += dot(lf[0, h * HALF : (h + 1) * HALF, :], down_leave[:, off : off + wide])
        for i in range(2):
            r_copy(c, h, i).wait_recv()
            total += tr[c, h, i, :, :wide].astype(F32)
        total = total.reshape(4, ROWS, wide)
        total = jnp.concatenate([total, jnp.zeros((4, PAD - ROWS, wide), F32)], axis=1)
        rows = total.astype(BF16)
        tp[c, 4 * h : 4 * h + 4, :, :wide] = rows
        for n in of_half(h):
            v_copy(c, n).start()
        if h == 0:
            vz[c, 0, :PAD, :wide] = rows[0]

    def stage_5(c):
        wide = OWN[c][1]
        for n in range(1, NZ):
            v_copy(c, n).wait_recv()
        rows = vz[c, :, :, :wide].reshape(NZ * 128, wide)
        mixed = dot(selwt[...], rows).reshape(NY, 128, wide)[:, :BLOCK]
        for m in range(1, NY):
            ys[c, m, :, :wide] = mixed[m].astype(BF16)
            o_copy(c, m).start()
        own[c, :, :wide] = mixed[0]

    def stage_6(c):
        off, wide = OWN[c]
        total = own[c, :, :wide]
        for m in range(1, NY):
            o_copy(c, m).wait_recv()
            total += yr[c, m, :, :wide].astype(F32)
        total = total.astype(BF16)
        for s in range(STEPS):
            out[s, :, off : off + wide] = total[s * TOK : (s + 1) * TOK]

    for m in range(1, NY):
        table_copy(m).start()
    tab[0] = table[y]
    stages = {
        "T": stage_tables, "y": stage_y, "B": stage_b, "b": stage_b2, "C": stage_c, "D": stage_d,
        "G": stage_g, "e": stage_e, "E": stage_e2, "H": stage_hidden, "P": stage_1, "Q": stage_2, "R": stage_3,
        "S": stage_4, "U": stage_5, "V": stage_6,
    }
    def sent_out(c):
        for m in range(1, NY):
            y_copy(c, m).wait_send()
        for n in range(1, NZ):
            z_copy(c, n).wait_send()
        for h in range(NH):
            for i in range(2):
                near(c, h, i, xp, x).wait_send()
                far(c, h, 2 + i, xp, x).wait_send()
                h_copy(c, h, i).wait_send()
            cross(c, h, core).wait_send()
            b_copy(c, h).wait_send()

    def sent_back(c, h):
        for i in range(2):
            r_copy(c, h, i).wait_send()
        for n in of_half(h):
            v_copy(c, n).wait_send()

    for name in ORDER:
        numbers = [int(n) for n in name[1:].split(".") if n]
        if name[0] == "M":
            stage_low(numbers[0], 0, numbers[1])
        else:
            if name[0] == "S" and numbers[1] == 1:
                sent_out(numbers[0])
                sent_back(numbers[0], 0)
            stages[name[0]](*numbers)
            if name[0] == "V":
                sent_back(numbers[0], 1)

    for kind in range(4):
        enter_copy(kind, xp, x).wait_send()
    enter_cross(core).wait_send()
    for m in range(1, NY):
        table_copy(m).wait_send()
    for h in range(NH):
        pair_copy(0, h).wait_send()
        back_copy(0, h, core).wait_send()
        for j in range(1, NX):
            low_copy(0, h, j).wait_send()
    for c in range(NC):
        for m in range(1, NY):
            o_copy(c, m).wait_send()


def on_device(
    tokens,
    routes,
    route_weights,
    domains,
    gate_weight,
    up_weight,
    down_weight,
    up_entry,
    up_exit,
    down_entry,
    down_exit,
):
    any_spec = pl.BlockSpec(memory_space=pl.ANY)
    vmem_spec = pl.BlockSpec(memory_space=pltpu.VMEM)
    dma = pltpu.SemaphoreType.DMA
    vmem = pltpu.VMEM
    return pl.pallas_call(
        kernel,
        out_shape=jax.ShapeDtypeStruct((STEPS, TOK, PART), BF16),
        in_specs=[any_spec] + [vmem_spec] * 3 + [any_spec] * 4 + [vmem_spec] * 3,
        out_specs=vmem_spec,
        scratch_shapes=[
            [vmem((8, wide, 2 * FFL), BF16) for _, wide in OWN],
            vmem((2 * NX, PART, LOW), BF16),
            vmem((FFL, D), BF16),
            vmem((NC, NY, 128, W), BF16),
            vmem((128, 128), F32),
            vmem((NY, 2 * NZ, 128), F32),
            vmem((NY, 2 * NZ, 128), F32),
            vmem((NZ * PAD, NY * 128), BF16),
            vmem((NY * 128, NZ * 128), BF16),
            vmem((NC, NZ, PAD, W), BF16),
            vmem((NC, NZ, PAD, W), BF16),
            [vmem((ALL, 8 * wide), BF16) for _, wide in OWN],
            vmem((ALL, LOW), BF16),
            vmem((ALL, 2 * FFL), F32),
            vmem((ALL, LOW), F32),
            vmem((ALL, FFL), BF16),
            vmem((1, ALL, LOW), BF16),
            vmem((1, NH, QUART, LOW), BF16),
            vmem((1, NH, NX, QUART, LOW), BF16),
            vmem((1, ALL, LOW), BF16),
            vmem((NC, NX, ALL, WIDE), BF16),
            vmem((NC, NX, ALL, WIDE), BF16),
            vmem((NC, NH, 3, HALF, WIDE), BF16),
            vmem((NC, NH, 2, QUART, WIDE), BF16),
            vmem((NC, NH, 2, HALF, WIDE), BF16),
            vmem((NC, NZ, PAD, WIDE), BF16),
            vmem((NC, NZ, 128, WIDE), BF16),
            vmem((NC, BLOCK, WIDE), F32),
            vmem((NC, NY, BLOCK, WIDE), BF16),
            vmem((NC, NY, BLOCK, WIDE), BF16),
            dma((6 * NC + 2,)),
            dma((5,)), dma((5,)),
            dma((NY,)), dma((NY,)),
            dma((NC * NY,)), dma((NC * NY,)),
            dma((NC * NZ,)), dma((NC * NZ,)),
            dma((NC * NH * 5,)), dma((NC * NH * 5,)),
            dma((NH * 8,)), dma((NH * 8,)),
            dma((NC * NH,)), dma((NC * NH,)),
            dma((NC * NH * 2,)), dma((NC * NH * 2,)),
            dma((NC * NH * 2,)), dma((NC * NH * 2,)),
            dma((NC * NZ,)), dma((NC * NZ,)),
            dma((NC * NY,)), dma((NC * NY,)),
        ],
        compiler_params=pltpu.CompilerParams(
            collective_id=0, has_side_effects=True, vmem_limit_bytes=62 * 1024 * 1024
        ),
        name="moe",
    )(
        tokens, routes, route_weights, domains,
        gate_weight[0].reshape(NX, 2, PART, FFL), up_weight[0].reshape(NX, 2, PART, FFL), down_weight[0],
        up_entry[0], up_exit[0], down_entry[0], down_exit[0],
    )


def solution(mesh):
    in_specs = (
        P(None, "expert", None),
        P(None, "expert", None),
        P(None, "expert", None),
        P(None, "expert"),
        P("expert", None, "dp"),
        P("expert", None, "dp"),
        P("expert", "dp", None),
        P("expert", "dp", None),
        P("expert", None, "dp"),
        P("expert", "dp", None),
        P("expert", None, "dp"),
    )
    out_specs = P(None, "expert", "dp")
    return jax.shard_map(
        on_device, mesh=mesh, in_specs=in_specs, out_specs=out_specs, check_vma=False
    )
```
